32 devices in a mesh: groups: 2 (over y), chan: 4 (over z), tm: 2 (over x), src: 2 (over core).
Axes of the slice: x: 2, y: 2, z: 4, core: 2. Of those that a mesh axis runs over, the one named last changes fastest.
Arguments:
- raw_records: bfloat16 [8, 4352, 512], P(('groups', 'tm', 'src'), 'chan'), parts along dimension 0, may hold values from -6 to 6
- filter_taps: float32 [64], replicated, may hold values from -0.75 to 0.75
- good_channels: int32 [1024], P(('groups', 'chan')), parts along dimension 0, may hold values 0 or 1
- source_ids: int32 [8, 4], P('groups'), parts along dimension 0, may hold values from 0 to 511
- window_offsets: int32 [8], P(('groups', 'tm', 'src')), parts along dimension 0, may hold values from 0 to 192, as said below
Outputs:
- correlations: float32 [32, 384, 512], P(('groups', 'tm', 'src'), None, 'chan'), parts along dimension 0
The draws below stay inside these ranges and needn't reach their ends.
There are 2 independent parts, one for each index of `groups`. The reference program is written for one: setup_inputs(seed, part) draws one part's arguments, and reference() takes and returns one part's arrays. A program takes and returns all parts, laid end to end along the dimension named above; an argument that names none is the same for every part. Nothing has to cross between parts.
Inputs may be any that keep to these rules, and one draw needn't show every extreme that they name: `window_offsets`: multiples of 4; in every part some window has offset 192.
All inputs are finite; a program needn't handle non-finite values. No bound on the sum of `good_channels` on one device may be relied on, other than what follows from the above.
Results may differ from the reference program's by a relative error of at most 0.0064.
Values may be sent and summed in bfloat16 or wider, within the bound.
A program may use at most 64 MiB of HBM per device.

```python
import math
import jax
import jax.numpy as jnp
from jax import lax

W = 1024
F = 512
TAPS = 64
BANDS = 8
LAGS = 384
SEG = 4352
STEPS = 4
NS = 4
NWIN = 4
CH = 512


def draw_window_offsets(key, part):
    first_key, second_key = jax.random.split(jax.random.fold_in(key, 11))
    steps_four = jax.random.randint(first_key, (NWIN,), 0, 49)
    chosen = jax.random.randint(second_key, (), 0, NWIN)
    steps_four = jnp.where(jnp.arange(NWIN) == chosen, 48, steps_four)
    return (4 * steps_four).astype(jnp.int32)


def with_ends(entries, stream_key, low, top_value):
    dims = entries.shape
    index_at = [jax.random.randint(jax.random.fold_in(stream_key, axis), (), 0, dims[axis]) for axis in range(len(dims))]
    entries = entries.at[tuple(index_at)].set(low)
    longest = dims.index(max(dims))
    index_at[longest] = (index_at[longest] + 1) % dims[longest]
    return entries.at[tuple(index_at)].set(top_value)


def block_scale(rng, shape, pieces, least, top_value):
    level = 1.0
    for axis_at, parts in pieces:
        draws = jax.random.uniform(jax.random.fold_in(jax.random.fold_in(rng, 6), axis_at), (parts,), jnp.float32, least / len(pieces), top_value / len(pieces))
        level = level * jnp.repeat(jnp.exp(draws), shape[axis_at] // parts).reshape((-1,) + (1,) * (len(shape) - 1 - axis_at))
    return level


def normal_values(rng, shape, width, limit, cuts=(), held_as=jnp.bfloat16):
    gain = block_scale(rng, shape, cuts, -0.22, 0.18) if cuts else 1.0
    drawn = jax.random.normal(rng, shape, jnp.float32) * width * gain
    return jnp.minimum(jnp.maximum(drawn, -limit), limit).astype(held_as)


def setup_inputs(seed: int = 0, part: int = 0) -> dict:
    seeds = jax.random.split(jax.random.key(seed), 6)
    own_keys = jax.random.split(jax.random.fold_in(seeds[5], part), 6)
    raw_records = normal_values(own_keys[0], (NWIN, SEG, CH), 1.0, 6.0, ((0, 4), (1, 4)))
    filter_taps = normal_values(seeds[1], (TAPS,), TAPS ** -0.5, 0.75, (), jnp.float32)
    good_channels = with_ends((jax.random.randint(own_keys[2], (CH,), 0, 10) < 9).astype(jnp.int32), jax.random.fold_in(own_keys[2], 1), 0, 1)
    source_ids = with_ends(jax.random.randint(own_keys[3], (STEPS, NS), 0, CH), jax.random.fold_in(own_keys[3], 1), 0, CH - 1).astype(jnp.int32)
    window_offsets = draw_window_offsets(jax.random.fold_in(jax.random.fold_in(seeds[5], part), 71), part)
    return {"raw_records": raw_records, "filter_taps": filter_taps, "good_channels": good_channels, "source_ids": source_ids, "window_offsets": window_offsets}


def forward_table(length, bins):
    sample = jnp.arange(length, dtype=jnp.int32)
    freq = jnp.arange(1, bins + 1, dtype=jnp.int32)
    phase = freq[:, None] * sample[None, :] % length
    angle = phase.astype(jnp.float32) * (2.0 * math.pi / length)
    return jnp.concatenate([jnp.cos(angle), -jnp.sin(angle)], axis=0).astype(jnp.bfloat16)

def inverse_table(length, bins, lag_count):
    freq = jnp.arange(1, bins + 1, dtype=jnp.int32)
    shift = jnp.arange(lag_count, dtype=jnp.int32) - lag_count // 2
    phase = jnp.mod(freq[:, None] * shift[None, :], length)
    angle = phase.astype(jnp.float32) * (2.0 * math.pi / length)
    return jnp.concatenate([jnp.cos(angle), -jnp.sin(angle)], axis=0)

def decimate(grouped, filter_taps):
    taps_four = filter_taps.reshape(-1, 4)
    count = grouped.shape[0] - taps_four.shape[0] + 1
    total = jnp.zeros((count, grouped.shape[2]), jnp.float32)
    for group in range(taps_four.shape[0]):
        total = total + lax.optimization_barrier(jnp.sum(grouped[group:group + count] * taps_four[group][None, :, None], axis=1))
    return total

def whiten(spectrum, keep):
    half = spectrum.shape[-2] // 2
    real_part = spectrum[..., :half, :]
    imag_part = spectrum[..., half:, :]
    shape = real_part.shape
    banded = shape[:-2] + (BANDS, half // BANDS, shape[-1])
    power = (real_part * real_part + imag_part * imag_part).reshape(banded)
    amp = jnp.sqrt(lax.optimization_barrier(jnp.mean(power, axis=-2, keepdims=True)) + 1e-06)
    factor = keep / amp
    real_out = (real_part.reshape(banded) * factor).reshape(shape)
    imag_out = (imag_part.reshape(banded) * factor).reshape(shape)
    return jnp.concatenate([real_out, imag_out], axis=-2).astype(jnp.bfloat16)

def reference(raw_records, filter_taps, good_channels, source_ids, window_offsets):
    table = forward_table(W, F)
    keep = good_channels.astype(jnp.float32)
    groups = TAPS // 4
    span = 4 * (W + groups - 1)

    def one_window(pair):
        record, offset = pair
        piece = lax.dynamic_slice_in_dim(record, offset, span, 0).astype(jnp.float32)
        filtered = decimate(piece.reshape(W + groups - 1, 4, CH), filter_taps).astype(jnp.bfloat16)
        spectrum = jnp.dot(table, filtered, preferred_element_type=jnp.float32)
        return whiten(spectrum, keep)
    spectra = lax.map(one_window, (raw_records, window_offsets))
    flat_ids = source_ids.reshape(-1).astype(jnp.int32)
    picked = jnp.moveaxis(jnp.take(spectra, flat_ids, axis=2), 2, 0)
    inverse = inverse_table(W, F, LAGS)
    scale = 1.0 / math.sqrt(NWIN * F)
    full = spectra.astype(jnp.float32)
    highest = lax.Precision.HIGHEST

    def one_source(source):
        values = source.astype(jnp.float32)
        src_real = values[:, :F]
        src_imag = values[:, F:]
        chan_real = full[:, :F, :]
        chan_imag = full[:, F:, :]
        cross_real = jnp.einsum('wf,wfc->fc', src_real, chan_real, precision=highest) + jnp.einsum('wf,wfc->fc', src_imag, chan_imag, precision=highest)
        cross_imag = jnp.einsum('wf,wfc->fc', src_real, chan_imag, precision=highest) - jnp.einsum('wf,wfc->fc', src_imag, chan_real, precision=highest)
        crosses = jnp.concatenate([cross_real, cross_imag], axis=0)
        return jnp.einsum('fl,fc->lc', inverse, crosses, precision=highest) * scale
    return lax.map(one_source, picked)
```

```python
import functools
import math

import jax
import jax.numpy as jnp
import ml_dtypes
import numpy as np
from jax import lax
from jax.experimental import pallas as pl
from jax.experimental.pallas import tpu as pltpu
from jax.sharding import PartitionSpec as P

W = 1024
F = 512
TAPS = 64
BANDS = 8
LAGS = 384
MAX_SHIFT = 48
NSRC = 16
LANES = 128
VMEM_LIMIT = 44 * 1024 * 1024
NT = (((1,), (1,)), ((), ()))


def up(value, step):
    return -(-value // step) * step


def layout(samples):
    count = samples // 4
    reach = TAPS // 4 - 1 + MAX_SHIFT
    used = up(count + reach, 16)
    rows = up(used, LANES)
    if used + rows // LANES * NSRC > rows:
        rows = up(used + rows // LANES * NSRC, LANES)
    return count, reach, used, rows


def waves(phase):
    angle = (phase % W).astype(np.float64) * (2.0 * math.pi / W)
    return np.concatenate([np.cos(angle), -np.sin(angle)], axis=0)


def forward_blocks(chans, samples):
    count, reach, used, rows = layout(samples)
    freq = np.arange(1, F + 1, dtype=np.int64)[:, None]
    parts = []
    for owner in range(chans):
        row = np.arange(rows, dtype=np.int64)
        sample = count * owner - reach + row
        inside = (sample >= 0) & (sample < W) & (row < used)
        parts.append(waves(freq * sample[None, :]) * inside[None, :])
    return np.concatenate(parts, axis=1).astype(np.float32).astype(ml_dtypes.bfloat16)


def inverse_rows():
    freq = np.arange(1, F + 1, dtype=np.int64)[:, None]
    shift = np.arange(LAGS, dtype=np.int64)[None, :] - LAGS // 2
    table = waves(freq * shift).astype(np.float32).T
    high = table.astype(ml_dtypes.bfloat16)
    low = (table - high.astype(np.float32)).astype(ml_dtypes.bfloat16)
    return np.ascontiguousarray(high), np.ascontiguousarray(low)


def gather_kernel(sizes, offset, taps, ids, keep, raw, out, toep, blocks, own_sem, send_sem, recv_sem):
    chans, tms, cores = sizes
    samples, channels = raw.shape
    count, reach, used, rows = layout(samples)
    here, tm, core = (lax.axis_index(name) for name in ("chan", "tm", "src"))
    window = tm * cores + core

    barrier = pltpu.get_barrier_semaphore()
    for axis, place, size in (("chan", here, chans), ("tm", tm, tms), ("src", core, cores)):
        for step in range(1, size):
            pl.semaphore_signal(
                barrier,
                inc=1,
                device_id={axis: lax.rem(place + step, size)},
                device_id_type=pl.DeviceIdType.MESH,
            )

    toep[...] = jnp.zeros_like(toep)
    row = lax.broadcasted_iota(jnp.int32, (32, 384), 0)
    col = lax.broadcasted_iota(jnp.int32, (32, 384), 1)
    tap_group = (col >> 2) - row - 1 - (offset[0] >> 2)
    base = jnp.zeros((32, 384), jnp.float32)
    for group in range(TAPS // 4):
        base = jnp.where(tap_group == group, taps[group : group + 1, :], base)
    high = base.astype(jnp.bfloat16)
    low = (base - high.astype(jnp.float32)).astype(jnp.bfloat16)
    for block in range(rows // 32):
        span = slice(128 * block, 128 * block + 384)
        toep[0, 32 * block : 32 * block + 32, span] = high
        toep[1, 32 * block : 32 * block + 32, span] = low
    lead = 4 * (reach + 1)
    samples_in = raw[...]
    total = jnp.dot(toep[0, :, lead : lead + samples], samples_in, preferred_element_type=jnp.float32)
    total += jnp.dot(toep[1, :, lead : lead + samples], samples_in, preferred_element_type=jnp.float32)
    filtered = total.astype(jnp.bfloat16)
    channel = lax.broadcasted_iota(jnp.int32, (NSRC, channels), 1)
    pick = jnp.where(channel == ids[...], 1.0, 0.0).astype(jnp.bfloat16)
    picked = lax.dot_general(pick, filtered, NT, preferred_element_type=jnp.float32).astype(jnp.bfloat16)
    keep_rows = jnp.broadcast_to(keep[...], (16, LANES)).astype(jnp.bfloat16)
    for owner in range(chans):
        blocks[owner, :used, :] = filtered[:used, owner * LANES : (owner + 1) * LANES]
        for tile in range((rows - used) // NSRC):
            at = used + tile * NSRC
            lanes = slice(tile * LANES, (tile + 1) * LANES)
            if tile < rows // LANES:
                blocks[owner, at : at + NSRC, :] = picked[:, lanes]
            else:
                blocks[owner, at : at + NSRC, :] = jnp.zeros((NSRC, LANES), jnp.bfloat16)
        blocks[owner, rows:, :] = keep_rows

    pl.semaphore_wait(barrier, chans + tms + cores - 3)

    sent = []

    def slot(part, owner):
        return out.at[part, owner]

    def send(source, part, owner, target):
        copy = pltpu.make_async_remote_copy(
            src_ref=source,
            dst_ref=slot(part, owner),
            send_sem=send_sem.at[len(sent)],
            recv_sem=recv_sem.at[part * chans + owner],
            device_id=target,
            device_id_type=pl.DeviceIdType.MESH,
        )
        copy.start()
        sent.append(copy)

    def arrive(part, owner):
        pltpu.make_async_remote_copy(
            src_ref=slot(part, owner),
            dst_ref=slot(part, owner),
            send_sem=send_sem.at[0],
            recv_sem=recv_sem.at[part * chans + owner],
            device_id={"chan": here},
            device_id_type=pl.DeviceIdType.MESH,
        ).wait_recv()

    def to_cores(part, owner):
        for step in range(1, cores):
            send(slot(part, owner), part, owner, {"src": lax.rem(core + step, cores)})

    for step in range(1, chans):
        there = lax.rem(here + step, chans)
        send(blocks.at[there], window, here, {"chan": there})
    own = pltpu.make_async_copy(blocks.at[here], slot(window, here), own_sem)
    own.start()
    own.wait()
    for step in range(chans):
        owner = lax.rem(here + chans - step, chans)
        if step:
            arrive(window, owner)
        for hop in range(1, tms):
            send(slot(window, owner), window, owner, {"tm": lax.rem(tm + hop, tms)})
        to_cores(window, owner)
    for step in range(chans):
        owner = lax.rem(here + chans - step, chans)
        for hop in range(1, tms):
            part = lax.rem(tm + tms - hop, tms) * cores + core
            arrive(part, owner)
            to_cores(part, owner)
    for step in range(chans):
        owner = lax.rem(here + chans - step, chans)
        for hop in range(tms):
            for turn in range(1, cores):
                part = lax.rem(tm + tms - hop, tms) * cores + lax.rem(core + turn, cores)
                arrive(part, owner)
    for copy in sent:
        copy.wait_send()


def correlate_kernel(sizes, samples, ids, keep, table, inv_high, inv_low, blocks, out, spec, src_spec, cross):
    chans, tms, cores = sizes
    windows = tms * cores
    _, _, used, rows = layout(samples)
    mine = NSRC // windows
    window = lax.axis_index("tm") * cores + lax.axis_index("src")
    width = 2 if windows % 2 == 0 else 1
    for first in range(0, windows, width):
        data = jnp.concatenate(
            [
                jnp.concatenate([blocks[part, owner, :rows, :] for owner in range(chans)], axis=0)
                for part in range(first, first + width)
            ],
            axis=1,
        )
        spec[:, first * LANES : (first + width) * LANES] = jnp.dot(
            table[...], data, preferred_element_type=jnp.float32
        )
    tiles = rows // LANES
    series = jnp.concatenate(
        [
            jnp.concatenate(
                [
                    blocks[part, owner, used + NSRC * tile : used + NSRC * (tile + 1), :]
                    for owner in range(chans)
                    for tile in range(tiles)
                ],
                axis=1,
            )
            for part in range(windows)
        ],
        axis=0,
    )
    src_spec[...] = lax.dot_general(table[...], series, NT, preferred_element_type=jnp.float32)

    channel = lax.broadcasted_iota(jnp.int32, (NSRC, LANES), 1)
    src_keep = jnp.zeros((NSRC, 1), jnp.float32)
    for owner in range(chans):
        flags = blocks[0, owner, rows : rows + 16, :].astype(jnp.float32)
        hit = channel + owner * LANES == ids[...]
        src_keep += jnp.sum(jnp.where(hit, flags, 0.0), axis=1, keepdims=True)
    number = lax.broadcasted_iota(jnp.int32, (NSRC, mine * LANES), 0)
    wanted = lax.broadcasted_iota(jnp.int32, (NSRC, mine * LANES), 1) // LANES + window * mine
    spread = (jnp.where(number == wanted, 1.0, 0.0) * src_keep).astype(jnp.bfloat16)
    keep_lanes = jnp.concatenate([keep[...]] * windows, axis=1)
    size = F // BANDS

    def whiten(real, imag, gain):
        power = jnp.mean(real * real + imag * imag, axis=0, keepdims=True)
        factor = gain / jnp.sqrt(power + 1e-06)
        return (real * factor).astype(jnp.bfloat16), (imag * factor).astype(jnp.bfloat16)

    @pl.loop(0, BANDS)
    def _(band):
        at_real = pl.ds(pl.multiple_of(band * size, size), size)
        at_imag = pl.ds(pl.multiple_of(F + band * size, size), size)
        real, imag = whiten(spec[at_real, :], spec[at_imag, :], keep_lanes)
        real, imag = real.astype(jnp.float32), imag.astype(jnp.float32)
        src = jnp.concatenate(
            whiten(src_spec[at_real, :], src_spec[at_imag, :], 1.0), axis=0
        )
        cross_real = [0.0] * mine
        cross_imag = [0.0] * mine
        for part in range(windows):
            wide = jnp.dot(
                src[:, part * NSRC : (part + 1) * NSRC], spread, preferred_element_type=jnp.float32
            )
            xr = real[:, part * LANES : (part + 1) * LANES]
            xi = imag[:, part * LANES : (part + 1) * LANES]
            for one in range(mine):
                sr = wide[:size, one * LANES : (one + 1) * LANES]
                si = wide[size:, one * LANES : (one + 1) * LANES]
                cross_real[one] = cross_real[one] + (sr * xr + si * xi)
                cross_imag[one] = cross_imag[one] + (sr * xi - si * xr)
        for one in range(mine):
            lanes = slice(one * LANES, (one + 1) * LANES)
            for at, value in ((at_real, cross_real[one]), (at_imag, cross_imag[one])):
                high = value.astype(jnp.bfloat16)
                cross[0, at, lanes] = high
                cross[1, at, lanes] = (value - high.astype(jnp.float32)).astype(jnp.bfloat16)

    scale = 1.0 / math.sqrt(windows * F)
    total = jnp.dot(inv_high[...], cross[0], preferred_element_type=jnp.float32)
    total += jnp.dot(inv_high[...], cross[1], preferred_element_type=jnp.float32)
    total += jnp.dot(inv_low[...], cross[0], preferred_element_type=jnp.float32)
    for one in range(mine):
        out[one] = total[:, one * LANES : (one + 1) * LANES] * scale


def body(sizes, table, inv_high, inv_low, raw_records, filter_taps, good_channels, source_ids, window_offsets):
    chans, tms, cores = sizes
    windows = tms * cores
    samples, channels = raw_records.shape[1:]
    count, reach, used, rows = layout(samples)
    ids = source_ids.reshape(NSRC, 1)
    keep = good_channels.astype(jnp.float32).reshape(1, LANES)
    taps = jnp.tile(filter_taps.reshape(TAPS // 4, 4), (1, 96))
    vmem = pl.BlockSpec(memory_space=pltpu.VMEM)
    smem = pl.BlockSpec(memory_space=pltpu.SMEM)
    copies = chans - 1 + chans * (tms - 1 + cores - 1 + (tms - 1) * (cores - 1))
    gathered = pl.pallas_call(
        functools.partial(gather_kernel, sizes),
        out_shape=jax.ShapeDtypeStruct((windows, chans, rows + 16, LANES), jnp.bfloat16),
        in_specs=[smem, vmem, vmem, vmem, vmem],
        out_specs=vmem,
        scratch_shapes=[
            pltpu.VMEM((2, rows, 4 * rows + 256), jnp.bfloat16),
            pltpu.VMEM((chans, rows + 16, LANES), jnp.bfloat16),
            pltpu.SemaphoreType.DMA,
            pltpu.SemaphoreType.DMA((copies,)),
            pltpu.SemaphoreType.DMA((windows * chans,)),
        ],
        compiler_params=pltpu.CompilerParams(
            collective_id=0, has_side_effects=True, vmem_limit_bytes=VMEM_LIMIT
        ),
        name="gather",
    )(window_offsets, taps, ids, keep, raw_records.reshape(samples, channels))
    mine = NSRC // windows
    return pl.pallas_call(
        functools.partial(correlate_kernel, sizes, samples),
        out_shape=jax.ShapeDtypeStruct((mine, LAGS, LANES), jnp.float32),
        in_specs=[vmem] * 6,
        out_specs=vmem,
        scratch_shapes=[
            pltpu.VMEM((2 * F, windows * LANES), jnp.float32),
            pltpu.VMEM((2 * F, windows * NSRC), jnp.float32),
            pltpu.VMEM((2, 2 * F, mine * LANES), jnp.bfloat16),
        ],
        compiler_params=pltpu.CompilerParams(vmem_limit_bytes=VMEM_LIMIT),
        name="correlate",
    )(ids, keep, table, inv_high, inv_low, gathered)


def solution(mesh):
    placed = (
        P(("groups", "tm", "src"), "chan", None),
        P(),
        P(("groups", "chan")),
        P("groups", None),
        P(("groups", "tm", "src")),
    )
    sizes = tuple(mesh.shape[name] for name in ("chan", "tm", "src"))

    def run(raw_records, *rest):
        table = forward_blocks(sizes[0], raw_records.shape[1])
        inv_high, inv_low = inverse_rows()
        return body(sizes, table, inv_high, inv_low, raw_records, *rest)

    def call(raw_records, *rest):
        return jax.shard_map(
            run,
            mesh=mesh,
            in_specs=placed,
            out_specs=P(("groups", "tm", "src"), None, "chan"),
            check_vma=False,
        )(raw_records, *rest)

    return call
```

```python
import functools
import math

import jax
import jax.numpy as jnp
import ml_dtypes
import numpy as np
from jax import lax
from jax.experimental import pallas as pl
from jax.experimental.pallas import tpu as pltpu
from jax.sharding import PartitionSpec as P

W = 1024
F = 512
TAPS = 64
BANDS = 8
LAGS = 384
MAX_SHIFT = 48
NSRC = 16
LANES = 128
GATHER_VMEM = 24 * 1024 * 1024
CORRELATE_VMEM = 48 * 1024 * 1024
NT = (((1,), (1,)), ((), ()))


def up(value, step):
    return -(-value // step) * step


def layout(samples):
    count = samples // 4
    reach = TAPS // 4 - 1 + MAX_SHIFT
    used = up(count + reach, 16)
    rows = up(used, LANES)
    if used + rows // LANES * NSRC > rows:
        rows = up(used + rows // LANES * NSRC, LANES)
    return count, reach, used, rows


def waves(phase):
    angle = (phase % W).astype(np.float64) * (2.0 * math.pi / W)
    return np.concatenate([np.cos(angle), -np.sin(angle)], axis=0)


def forward_blocks(chans, samples):
    count, reach, used, rows = layout(samples)
    freq = np.arange(1, F + 1, dtype=np.int64)[:, None]
    parts = []
    for owner in range(chans):
        row = np.arange(rows, dtype=np.int64)
        sample = count * owner - reach + row
        inside = (sample >= 0) & (sample < W) & (row < used)
        parts.append(waves(freq * sample[None, :]) * inside[None, :])
    return np.concatenate(parts, axis=1).astype(np.float32).astype(ml_dtypes.bfloat16)


def inverse_rows():
    freq = np.arange(1, F + 1, dtype=np.int64)[:, None]
    shift = np.arange(LAGS, dtype=np.int64)[None, :] - LAGS // 2
    table = waves(freq * shift).astype(np.float32).T
    high = table.astype(ml_dtypes.bfloat16)
    low = (table - high.astype(np.float32)).astype(ml_dtypes.bfloat16)
    return np.ascontiguousarray(high), np.ascontiguousarray(low)


def id_column(ids):
    number = lax.broadcasted_iota(jnp.int32, (NSRC, 1), 0)
    column = jnp.zeros((NSRC, 1), jnp.int32)
    per_step = ids.shape[1]
    for source in range(NSRC):
        column = jnp.where(number == source, ids[source // per_step, source % per_step], column)
    return column


def gather_kernel(
    sizes, offset, taps, ids, keep, raw_hbm, out, raw, toep, blocks, raw_sem, own_sem, send_sem, recv_sem
):
    read = pltpu.make_async_copy(raw_hbm, raw, raw_sem)
    read.start()
    chans, tms, cores = sizes
    samples, channels = raw.shape
    count, reach, used, rows = layout(samples)
    here, tm, core = (lax.axis_index(name) for name in ("chan", "tm", "src"))
    window = tm * cores + core

    barrier = pltpu.get_barrier_semaphore()
    for axis, place, size in (("chan", here, chans), ("tm", tm, tms), ("src", core, cores)):
        for step in range(1, size):
            pl.semaphore_signal(
                barrier,
                inc=1,
                device_id={axis: lax.rem(place + step, size)},
                device_id_type=pl.DeviceIdType.MESH,
            )

    toep[...] = jnp.zeros_like(toep)
    row = lax.broadcasted_iota(jnp.int32, (32, 384), 0)
    col = lax.broadcasted_iota(jnp.int32, (32, 384), 1)
    tap_at = col - 4 * row - 4 - offset[0]
    base = jnp.zeros((32, 384), jnp.float32)
    for tap in range(TAPS):
        base = jnp.where(tap_at == tap, taps[tap], base)
    high = base.astype(jnp.bfloat16)
    low = (base - high.astype(jnp.float32)).astype(jnp.bfloat16)
    for block in range(rows // 32):
        span = slice(128 * block, 128 * block + 384)
        toep[0, 32 * block : 32 * block + 32, span] = high
        toep[1, 32 * block : 32 * block + 32, span] = low
    lead = 4 * (reach + 1)
    read.wait()
    samples_in = raw[...]
    total = jnp.dot(toep[0, :, lead : lead + samples], samples_in, preferred_element_type=jnp.float32)
    total += jnp.dot(toep[1, :, lead : lead + samples], samples_in, preferred_element_type=jnp.float32)
    filtered = total.astype(jnp.bfloat16)
    channel = lax.broadcasted_iota(jnp.int32, (NSRC, channels), 1)
    pick = jnp.where(channel == id_column(ids), 1.0, 0.0).astype(jnp.bfloat16)
    picked = lax.dot_general(pick, filtered, NT, preferred_element_type=jnp.float32).astype(jnp.bfloat16)
    keep_rows = jnp.broadcast_to(keep[...].astype(jnp.float32), (16, LANES)).astype(jnp.bfloat16)
    for owner in range(chans):
        blocks[owner, :used, :] = filtered[:used, owner * LANES : (owner + 1) * LANES]
        for tile in range((rows - used) // NSRC):
            at = used + tile * NSRC
            lanes = slice(tile * LANES, (tile + 1) * LANES)
            if tile < rows // LANES:
                blocks[owner, at : at + NSRC, :] = picked[:, lanes]
            else:
                blocks[owner, at : at + NSRC, :] = jnp.zeros((NSRC, LANES), jnp.bfloat16)
        blocks[owner, rows:, :] = keep_rows

    pl.semaphore_wait(barrier, chans + tms + cores - 3)

    sent = []

    def slot(part, owner):
        return out.at[part, owner]

    def send(source, part, owner, target):
        copy = pltpu.make_async_remote_copy(
            src_ref=source,
            dst_ref=slot(part, owner),
            send_sem=send_sem.at[len(sent)],
            recv_sem=recv_sem.at[part * chans + owner],
            device_id=target,
            device_id_type=pl.DeviceIdType.MESH,
        )
        copy.start()
        sent.append(copy)

    def arrive(part, owner):
        pltpu.make_async_remote_copy(
            src_ref=slot(part, owner),
            dst_ref=slot(part, owner),
            send_sem=send_sem.at[0],
            recv_sem=recv_sem.at[part * chans + owner],
            device_id={"chan": here},
            device_id_type=pl.DeviceIdType.MESH,
        ).wait_recv()

    def to_cores(part, owner):
        for step in range(1, cores):
            send(slot(part, owner), part, owner, {"src": lax.rem(core + step, cores)})

    for step in range(1, chans):
        there = lax.rem(here + step, chans)
        send(blocks.at[there], window, here, {"chan": there})
    own = pltpu.make_async_copy(blocks.at[here], slot(window, here), own_sem)
    own.start()
    for step in range(chans):
        owner = lax.rem(here + chans - step, chans)
        if step:
            arrive(window, owner)
        source = slot(window, owner) if step else blocks.at[here]
        for hop in range(1, tms):
            send(source, window, owner, {"tm": lax.rem(tm + hop, tms)})
        for turn in range(1, cores):
            send(source, window, owner, {"src": lax.rem(core + turn, cores)})
    own.wait()
    for step in range(chans):
        owner = lax.rem(here + chans - step, chans)
        for hop in range(1, tms):
            part = lax.rem(tm + tms - hop, tms) * cores + core
            arrive(part, owner)
            to_cores(part, owner)
    for step in range(chans):
        owner = lax.rem(here + chans - step, chans)
        for hop in range(tms):
            for turn in range(1, cores):
                part = lax.rem(tm + tms - hop, tms) * cores + lax.rem(core + turn, cores)
                arrive(part, owner)
    for copy in sent:
        copy.wait_send()


def correlate_kernel(
    sizes, samples, ids, keep, table_hbm, high_hbm, low_hbm, blocks, out, spec, src_spec, cross, tables, inv_high, inv_low, sems
):
    quarter = F // 2
    table_reads = [
        pltpu.make_async_copy(table_hbm.at[pl.ds(part * quarter, quarter)], tables.at[part], sems.at[2 + part])
        for part in range(4)
    ]
    for read in table_reads:
        read.start()
    reads = [
        pltpu.make_async_copy(high_hbm, inv_high, sems.at[0]),
        pltpu.make_async_copy(low_hbm, inv_low, sems.at[1]),
    ]
    for read in reads:
        read.start()
    chans, tms, cores = sizes
    windows = tms * cores
    _, _, used, rows = layout(samples)
    mine = NSRC // windows
    window = lax.axis_index("tm") * cores + lax.axis_index("src")
    width = 2 if windows % 2 == 0 else 1
    pairs = [
        jnp.concatenate(
            [
                jnp.concatenate([blocks[part, owner, :rows, :] for owner in range(chans)], axis=0)
                for part in range(first, first + width)
            ],
            axis=1,
        )
        for first in range(0, windows, width)
    ]
    tiles = rows // LANES
    series = jnp.concatenate(
        [
            jnp.concatenate(
                [
                    blocks[part, owner, used + NSRC * tile : used + NSRC * (tile + 1), :]
                    for owner in range(chans)
                    for tile in range(tiles)
                ],
                axis=1,
            )
            for part in range(windows)
        ],
        axis=0,
    )
    for number, read in enumerate(table_reads):
        read.wait()
        table = tables[number]
        at = slice(number * quarter, (number + 1) * quarter)
        for pair, data in enumerate(pairs):
            lanes = slice(pair * width * LANES, (pair + 1) * width * LANES)
            spec[at, lanes] = jnp.dot(table, data, preferred_element_type=jnp.float32)
        src_spec[at, :] = lax.dot_general(table, series, NT, preferred_element_type=jnp.float32)

    channel = lax.broadcasted_iota(jnp.int32, (NSRC, LANES), 1)
    id_at = id_column(ids)
    src_keep = jnp.zeros((NSRC, 1), jnp.float32)
    for owner in range(chans):
        flags = blocks[0, owner, rows : rows + 16, :].astype(jnp.float32)
        hit = channel + owner * LANES == id_at
        src_keep += jnp.sum(jnp.where(hit, flags, 0.0), axis=1, keepdims=True)
    number = lax.broadcasted_iota(jnp.int32, (NSRC, mine * LANES), 0)
    wanted = lax.broadcasted_iota(jnp.int32, (NSRC, mine * LANES), 1) // LANES + window * mine
    spread = (jnp.where(number == wanted, 1.0, 0.0) * src_keep).astype(jnp.bfloat16)
    keep_lanes = jnp.concatenate([keep[...].astype(jnp.float32)] * windows, axis=1)
    size = F // BANDS

    def whiten(real, imag, gain):
        power = jnp.mean(real * real + imag * imag, axis=0, keepdims=True)
        factor = gain / jnp.sqrt(power + 1e-06)
        return (real * factor).astype(jnp.bfloat16), (imag * factor).astype(jnp.bfloat16)

    @pl.loop(0, BANDS)
    def _(band):
        at_real = pl.ds(pl.multiple_of(band * size, size), size)
        at_imag = pl.ds(pl.multiple_of(F + band * size, size), size)
        real, imag = whiten(spec[at_real, :], spec[at_imag, :], keep_lanes)
        real, imag = real.astype(jnp.float32), imag.astype(jnp.float32)
        src = jnp.concatenate(
            whiten(src_spec[at_real, :], src_spec[at_imag, :], 1.0), axis=0
        )
        cross_real = [0.0] * mine
        cross_imag = [0.0] * mine
        for part in range(windows):
            wide = jnp.dot(
                src[:, part * NSRC : (part + 1) * NSRC], spread, preferred_element_type=jnp.float32
            )
            xr = real[:, part * LANES : (part + 1) * LANES]
            xi = imag[:, part * LANES : (part + 1) * LANES]
            for one in range(mine):
                sr = wide[:size, one * LANES : (one + 1) * LANES]
                si = wide[size:, one * LANES : (one + 1) * LANES]
                cross_real[one] = cross_real[one] + (sr * xr + si * xi)
                cross_imag[one] = cross_imag[one] + (sr * xi - si * xr)
        for one in range(mine):
            lanes = slice(one * LANES, (one + 1) * LANES)
            for at, value in ((at_real, cross_real[one]), (at_imag, cross_imag[one])):
                high = value.astype(jnp.bfloat16)
                cross[0, at, lanes] = high
                cross[1, at, lanes] = (value - high.astype(jnp.float32)).astype(jnp.bfloat16)

    scale = 1.0 / math.sqrt(windows * F)
    for read in reads:
        read.wait()
    total = jnp.dot(inv_high[...], cross[0], preferred_element_type=jnp.float32)
    total += jnp.dot(inv_high[...], cross[1], preferred_element_type=jnp.float32)
    total += jnp.dot(inv_low[...], cross[0], preferred_element_type=jnp.float32)
    for one in range(mine):
        out[one] = total[:, one * LANES : (one + 1) * LANES] * scale


def body(sizes, table, inv_high, inv_low, raw_records, filter_taps, good_channels, source_ids, window_offsets):
    chans, tms, cores = sizes
    windows = tms * cores
    samples, channels = raw_records.shape[1:]
    count, reach, used, rows = layout(samples)
    keep = good_channels.reshape(1, LANES)
    vmem = pl.BlockSpec(memory_space=pltpu.VMEM)
    smem = pl.BlockSpec(memory_space=pltpu.SMEM)
    hbm = pl.BlockSpec(memory_space=pltpu.HBM)
    copies = chans - 1 + chans * (tms - 1 + cores - 1 + (tms - 1) * (cores - 1))
    gathered = pl.pallas_call(
        functools.partial(gather_kernel, sizes),
        out_shape=jax.ShapeDtypeStruct((windows, chans, rows + 16, LANES), jnp.bfloat16),
        in_specs=[smem, smem, smem, vmem, hbm],
        out_specs=vmem,
        scratch_shapes=[
            pltpu.VMEM((samples, channels), jnp.bfloat16),
            pltpu.VMEM((2, rows, 4 * rows + 256), jnp.bfloat16),
            pltpu.VMEM((chans, rows + 16, LANES), jnp.bfloat16),
            pltpu.SemaphoreType.DMA,
            pltpu.SemaphoreType.DMA,
            pltpu.SemaphoreType.DMA((copies,)),
            pltpu.SemaphoreType.DMA((windows * chans,)),
        ],
        compiler_params=pltpu.CompilerParams(
            collective_id=0, has_side_effects=True, vmem_limit_bytes=GATHER_VMEM
        ),
        name="gather",
    )(window_offsets, filter_taps, source_ids, keep, raw_records.reshape(samples, channels))
    mine = NSRC // windows
    return pl.pallas_call(
        functools.partial(correlate_kernel, sizes, samples),
        out_shape=jax.ShapeDtypeStruct((mine, LAGS, LANES), jnp.float32),
        in_specs=[smem, vmem, hbm, hbm, hbm, vmem],
        out_specs=vmem,
        scratch_shapes=[
            pltpu.VMEM((2 * F, windows * LANES), jnp.float32),
            pltpu.VMEM((2 * F, windows * NSRC), jnp.float32),
            pltpu.VMEM((2, 2 * F, mine * LANES), jnp.bfloat16),
            pltpu.VMEM((4, F // 2, table.shape[1]), jnp.bfloat16),
            pltpu.VMEM((LAGS, 2 * F), jnp.bfloat16),
            pltpu.VMEM((LAGS, 2 * F), jnp.bfloat16),
            pltpu.SemaphoreType.DMA((6,)),
        ],
        compiler_params=pltpu.CompilerParams(vmem_limit_bytes=CORRELATE_VMEM),
        name="correlate",
    )(source_ids, keep, table, inv_high, inv_low, gathered)


def solution(mesh):
    placed = (
        P(("groups", "tm", "src"), "chan", None),
        P(),
        P(("groups", "chan")),
        P("groups", None),
        P(("groups", "tm", "src")),
    )
    sizes = tuple(mesh.shape[name] for name in ("chan", "tm", "src"))

    def run(raw_records, *rest):
        table = forward_blocks(sizes[0], raw_records.shape[1])
        inv_high, inv_low = inverse_rows()
        return body(sizes, table, inv_high, inv_low, raw_records, *rest)

    def call(raw_records, *rest):
        return jax.shard_map(
            run,
            mesh=mesh,
            in_specs=placed,
            out_specs=P(("groups", "tm", "src"), None, "chan"),
            check_vma=False,
        )(raw_records, *rest)

    return call
```

```python
import functools
import math

import jax
import jax.numpy as jnp
import ml_dtypes
import numpy as np
from jax import lax
from jax.experimental import pallas as pl
from jax.experimental.pallas import tpu as pltpu
from jax.sharding import PartitionSpec as P

W = 1024
F = 512
TAPS = 64
BANDS = 8
LAGS = 384
MAX_SHIFT = 48
NSRC = 16
LANES = 128
VMEM_LIMIT = 44 * 1024 * 1024
NT = (((1,), (1,)), ((), ()))


def up(value, step):
    return -(-value // step) * step


def layout(samples):
    count = samples // 4
    reach = TAPS // 4 + MAX_SHIFT
    used = up(count + reach, 16)
    rows = up(used, LANES)
    if used + rows // LANES * NSRC > rows:
        rows = up(used + rows // LANES * NSRC, LANES)
    return count, reach, used, rows


def waves(phase):
    angle = (phase % W).astype(np.float64) * (2.0 * math.pi / W)
    return np.concatenate([np.cos(angle), -np.sin(angle)], axis=0)


def forward_rows():
    freq = np.arange(1, F + 1, dtype=np.int64)[:, None]
    table = waves(freq * np.arange(W, dtype=np.int64)[None, :])
    return table.astype(np.float32).astype(ml_dtypes.bfloat16)


def inverse_rows():
    freq = np.arange(1, F + 1, dtype=np.int64)[:, None]
    shift = np.arange(LAGS, dtype=np.int64)[None, :] - LAGS // 2
    table = waves(freq * shift).astype(np.float32).T
    return np.ascontiguousarray(table.astype(ml_dtypes.bfloat16))


def gather_kernel(sizes, offset, taps, ids, keep, raw, out, toep, blocks, own_sem, send_sem, recv_sem):
    chans, tms, cores = sizes
    samples, channels = raw.shape
    count, reach, used, rows = layout(samples)
    here, tm, core = (lax.axis_index(name) for name in ("chan", "tm", "src"))
    window = tm * cores + core

    barrier = pltpu.get_barrier_semaphore()
    for axis, place, size in (("chan", here, chans), ("tm", tm, tms), ("src", core, cores)):
        for step in range(1, size):
            pl.semaphore_signal(
                barrier,
                inc=1,
                device_id={axis: lax.rem(place + step, size)},
                device_id_type=pl.DeviceIdType.MESH,
            )

    toep[...] = jnp.zeros_like(toep)
    row = lax.broadcasted_iota(jnp.int32, (32, 384), 0)
    col = lax.broadcasted_iota(jnp.int32, (32, 384), 1)
    tap_group = (col >> 2) - row - (offset[0] >> 2)
    base = jnp.zeros((32, 384), jnp.float32)
    for group in range(TAPS // 4):
        base = jnp.where(tap_group == group, taps[group : group + 1, :], base)
    high = base.astype(jnp.bfloat16)
    low = (base - high.astype(jnp.float32)).astype(jnp.bfloat16)
    for block in range(rows // 32):
        span = slice(128 * block, 128 * block + 384)
        toep[0, 32 * block : 32 * block + 32, span] = high
        toep[1, 32 * block : 32 * block + 32, span] = low
    lead = 4 * reach
    samples_in = raw[...]
    total = jnp.dot(toep[0, :, lead : lead + samples], samples_in, preferred_element_type=jnp.float32)
    total += jnp.dot(toep[1, :, lead : lead + samples], samples_in, preferred_element_type=jnp.float32)
    filtered = total.astype(jnp.bfloat16)
    channel = lax.broadcasted_iota(jnp.int32, (NSRC, channels), 1)
    pick = jnp.where(channel == ids[...], 1.0, 0.0).astype(jnp.bfloat16)
    picked = lax.dot_general(pick, filtered, NT, preferred_element_type=jnp.float32).astype(jnp.bfloat16)
    keep_rows = jnp.broadcast_to(keep[...], (16, LANES)).astype(jnp.bfloat16)
    for owner in range(chans):
        blocks[owner, :used, :] = filtered[:used, owner * LANES : (owner + 1) * LANES]
        for tile in range((rows - used) // NSRC):
            at = used + tile * NSRC
            lanes = slice(tile * LANES, (tile + 1) * LANES)
            if tile < rows // LANES:
                blocks[owner, at : at + NSRC, :] = picked[:, lanes]
            else:
                blocks[owner, at : at + NSRC, :] = jnp.zeros((NSRC, LANES), jnp.bfloat16)
        blocks[owner, rows:, :] = keep_rows

    pl.semaphore_wait(barrier, chans + tms + cores - 3)

    sent = []

    def slot(part, owner):
        return out.at[part, owner]

    def send(source, part, owner, target):
        copy = pltpu.make_async_remote_copy(
            src_ref=source,
            dst_ref=slot(part, owner),
            send_sem=send_sem.at[len(sent)],
            recv_sem=recv_sem.at[part * chans + owner],
            device_id=target,
            device_id_type=pl.DeviceIdType.MESH,
        )
        copy.start()
        sent.append(copy)

    def arrive(part, owner):
        pltpu.make_async_remote_copy(
            src_ref=slot(part, owner),
            dst_ref=slot(part, owner),
            send_sem=send_sem.at[0],
            recv_sem=recv_sem.at[part * chans + owner],
            device_id={"chan": here},
            device_id_type=pl.DeviceIdType.MESH,
        ).wait_recv()

    def to_cores(part, owner):
        for step in range(1, cores):
            send(slot(part, owner), part, owner, {"src": lax.rem(core + step, cores)})

    for step in range(1, chans):
        there = lax.rem(here + step, chans)
        send(blocks.at[there], window, here, {"chan": there})
    own = pltpu.make_async_copy(blocks.at[here], slot(window, here), own_sem)
    own.start()
    for step in range(chans):
        owner = lax.rem(here + chans - step, chans)
        if step:
            arrive(window, owner)
        source = slot(window, owner) if step else blocks.at[here]
        for hop in range(1, tms):
            send(source, window, owner, {"tm": lax.rem(tm + hop, tms)})
        for turn in range(1, cores):
            send(source, window, owner, {"src": lax.rem(core + turn, cores)})
    own.wait()
    for step in range(chans):
        owner = lax.rem(here + chans - step, chans)
        for hop in range(1, tms):
            part = lax.rem(tm + tms - hop, tms) * cores + core
            arrive(part, owner)
            to_cores(part, owner)
    for step in range(chans):
        owner = lax.rem(here + chans - step, chans)
        for hop in range(tms):
            for turn in range(1, cores):
                part = lax.rem(tm + tms - hop, tms) * cores + lax.rem(core + turn, cores)
                arrive(part, owner)
    for copy in sent:
        copy.wait_send()


def correlate_kernel(sizes, samples, ids, keep, table, inverse, blocks, out, spec, src_spec, cross, joined, src_joined):
    chans, tms, cores = sizes
    windows = tms * cores
    count, reach, used, rows = layout(samples)
    mine = NSRC // windows
    window = lax.axis_index("tm") * cores + lax.axis_index("src")
    width = 2 if windows % 2 == 0 else 1
    tiles = rows // LANES
    joined[...] = jnp.zeros_like(joined)
    src_joined[...] = jnp.zeros_like(src_joined)
    for owner in range(chans):
        at = slice(count * owner, count * owner + used)
        for part in range(windows):
            lanes = slice(part * LANES, (part + 1) * LANES)
            joined[at, lanes] += blocks[part, owner, :used, :].astype(jnp.float32)
        series = jnp.concatenate(
            [
                jnp.concatenate(
                    [blocks[part, owner, used + NSRC * tile : used + NSRC * (tile + 1), :] for tile in range(tiles)],
                    axis=1,
                )
                for part in range(windows)
            ],
            axis=0,
        ).astype(jnp.float32)
        src_joined[at, :] += series.T[:used, :]
    for first in range(0, windows, width):
        lanes = slice(first * LANES, (first + width) * LANES)
        data = joined[reach : reach + W, lanes].astype(jnp.bfloat16)
        spec[:, lanes] = jnp.dot(table[...], data, preferred_element_type=jnp.float32)
    data = src_joined[reach : reach + W, :].astype(jnp.bfloat16)
    src_spec[...] = jnp.dot(table[...], data, preferred_element_type=jnp.float32)

    channel = lax.broadcasted_iota(jnp.int32, (NSRC, LANES), 1)
    src_keep = jnp.zeros((NSRC, 1), jnp.float32)
    for owner in range(chans):
        flags = blocks[0, owner, rows : rows + 16, :].astype(jnp.float32)
        hit = channel + owner * LANES == ids[...]
        src_keep += jnp.sum(jnp.where(hit, flags, 0.0), axis=1, keepdims=True)
    number = lax.broadcasted_iota(jnp.int32, (NSRC, mine * LANES), 0)
    wanted = lax.broadcasted_iota(jnp.int32, (NSRC, mine * LANES), 1) // LANES + window * mine
    spread = (jnp.where(number == wanted, 1.0, 0.0) * src_keep).astype(jnp.bfloat16)
    keep_lanes = jnp.concatenate([keep[...]] * windows, axis=1)
    size = F // BANDS

    def whiten(real, imag, gain):
        power = jnp.mean(real * real + imag * imag, axis=0, keepdims=True)
        factor = gain / jnp.sqrt(power + 1e-06)
        return (real * factor).astype(jnp.bfloat16), (imag * factor).astype(jnp.bfloat16)

    @pl.loop(0, BANDS)
    def _(band):
        at_real = pl.ds(pl.multiple_of(band * size, size), size)
        at_imag = pl.ds(pl.multiple_of(F + band * size, size), size)
        real, imag = whiten(spec[at_real, :], spec[at_imag, :], keep_lanes)
        real, imag = real.astype(jnp.float32), imag.astype(jnp.float32)
        src = jnp.concatenate(
            whiten(src_spec[at_real, :], src_spec[at_imag, :], 1.0), axis=0
        )
        cross_real = [0.0] * mine
        cross_imag = [0.0] * mine
        for part in range(windows):
            wide = jnp.dot(
                src[:, part * NSRC : (part + 1) * NSRC], spread, preferred_element_type=jnp.float32
            )
            xr = real[:, part * LANES : (part + 1) * LANES]
            xi = imag[:, part * LANES : (part + 1) * LANES]
            for one in range(mine):
                sr = wide[:size, one * LANES : (one + 1) * LANES]
                si = wide[size:, one * LANES : (one + 1) * LANES]
                cross_real[one] = cross_real[one] + (sr * xr + si * xi)
                cross_imag[one] = cross_imag[one] + (sr * xi - si * xr)
        for one in range(mine):
            lanes = slice(one * LANES, (one + 1) * LANES)
            for at, value in ((at_real, cross_real[one]), (at_imag, cross_imag[one])):
                high = value.astype(jnp.bfloat16)
                cross[0, at, lanes] = high
                cross[1, at, lanes] = (value - high.astype(jnp.float32)).astype(jnp.bfloat16)

    scale = 1.0 / math.sqrt(windows * F)
    total = jnp.dot(inverse[...], cross[0], preferred_element_type=jnp.float32)
    total += jnp.dot(inverse[...], cross[1], preferred_element_type=jnp.float32)
    for one in range(mine):
        out[one] = total[:, one * LANES : (one + 1) * LANES] * scale


def body(sizes, table, inverse, raw_records, filter_taps, good_channels, source_ids, window_offsets):
    chans, tms, cores = sizes
    windows = tms * cores
    samples, channels = raw_records.shape[1:]
    count, reach, used, rows = layout(samples)
    ids = source_ids.reshape(NSRC, 1)
    keep = good_channels.astype(jnp.float32).reshape(1, LANES)
    taps = jnp.tile(filter_taps.reshape(TAPS // 4, 4), (1, 96))
    vmem = pl.BlockSpec(memory_space=pltpu.VMEM)
    smem = pl.BlockSpec(memory_space=pltpu.SMEM)
    copies = chans - 1 + chans * (tms - 1 + cores - 1 + (tms - 1) * (cores - 1))
    gathered = pl.pallas_call(
        functools.partial(gather_kernel, sizes),
        out_shape=jax.ShapeDtypeStruct((windows, chans, rows + 16, LANES), jnp.bfloat16),
        in_specs=[smem, vmem, vmem, vmem, vmem],
        out_specs=vmem,
        scratch_shapes=[
            pltpu.VMEM((2, rows, 4 * rows + 256), jnp.bfloat16),
            pltpu.VMEM((chans, rows + 16, LANES), jnp.bfloat16),
            pltpu.SemaphoreType.DMA,
            pltpu.SemaphoreType.DMA((copies,)),
            pltpu.SemaphoreType.DMA((windows * chans,)),
        ],
        compiler_params=pltpu.CompilerParams(
            collective_id=0, has_side_effects=True, vmem_limit_bytes=VMEM_LIMIT
        ),
        name="gather",
    )(window_offsets, taps, ids, keep, raw_records.reshape(samples, channels))
    mine = NSRC // windows
    return pl.pallas_call(
        functools.partial(correlate_kernel, sizes, samples),
        out_shape=jax.ShapeDtypeStruct((mine, LAGS, LANES), jnp.float32),
        in_specs=[vmem] * 5,
        out_specs=vmem,
        scratch_shapes=[
            pltpu.VMEM((2 * F, windows * LANES), jnp.float32),
            pltpu.VMEM((2 * F, windows * NSRC), jnp.float32),
            pltpu.VMEM((2, 2 * F, mine * LANES), jnp.bfloat16),
            pltpu.VMEM((up(count * (chans - 1) + used, 8), windows * LANES), jnp.float32),
            pltpu.VMEM((up(count * (chans - 1) + used, 8), windows * NSRC), jnp.float32),
        ],
        compiler_params=pltpu.CompilerParams(vmem_limit_bytes=VMEM_LIMIT),
        name="correlate",
    )(ids, keep, table, inverse, gathered)


def solution(mesh):
    placed = (
        P(("groups", "tm", "src"), "chan", None),
        P(),
        P(("groups", "chan")),
        P("groups", None),
        P(("groups", "tm", "src")),
    )
    sizes = tuple(mesh.shape[name] for name in ("chan", "tm", "src"))

    def run(raw_records, *rest):
        return body(sizes, forward_rows(), inverse_rows(), raw_records, *rest)

    def call(raw_records, *rest):
        return jax.shard_map(
            run,
            mesh=mesh,
            in_specs=placed,
            out_specs=P(("groups", "tm", "src"), None, "chan"),
            check_vma=False,
        )(raw_records, *rest)

    return call
```

```python
import functools
import math

import jax
import jax.numpy as jnp
import ml_dtypes
import numpy as np
from jax import lax
from jax.experimental import pallas as pl
from jax.experimental.pallas import tpu as pltpu
from jax.sharding import PartitionSpec as P

W = 1024
F = 512
TAPS = 64
BANDS = 8
LAGS = 384
MAX_SHIFT = 48
NSRC = 16
LANES = 128
VMEM_LIMIT = 44 * 1024 * 1024
NT = (((1,), (1,)), ((), ()))


def up(value, step):
    return -(-value // step) * step


def layout(samples):
    count = samples // 4
    reach = TAPS // 4
    used = up(count + reach, 16)
    rows = up(used, LANES)
    return count, reach, used, rows, used + rows // LANES * NSRC


def waves(phase):
    angle = (phase % W).astype(np.float64) * (2.0 * math.pi / W)
    return np.concatenate([np.cos(angle), -np.sin(angle)], axis=0)


def forward_rows():
    freq = np.arange(1, F + 1, dtype=np.int64)[:, None]
    table = waves(freq * np.arange(W, dtype=np.int64)[None, :])
    return table.astype(np.float32).astype(ml_dtypes.bfloat16)


def inverse_rows():
    freq = np.arange(1, F + 1, dtype=np.int64)[:, None]
    shift = np.arange(LAGS, dtype=np.int64)[None, :] - LAGS // 2
    table = waves(freq * shift).astype(np.float32).T
    return np.ascontiguousarray(table.astype(ml_dtypes.bfloat16))


def gather_kernel(sizes, offset, taps, ids, keep, raw, out, toep, blocks, own_sem, send_sem, recv_sem):
    chans, tms, cores = sizes
    samples, channels = raw.shape
    count, reach, used, rows, flag_row = layout(samples)
    here, tm, core = (lax.axis_index(name) for name in ("chan", "tm", "src"))
    window = tm * cores + core

    barrier = pltpu.get_barrier_semaphore()
    for axis, place, size in (("chan", here, chans), ("tm", tm, tms), ("src", core, cores)):
        for step in range(1, size):
            pl.semaphore_signal(
                barrier,
                inc=1,
                device_id={axis: lax.rem(place + step, size)},
                device_id_type=pl.DeviceIdType.MESH,
            )

    toep[...] = jnp.zeros_like(toep)
    row = lax.broadcasted_iota(jnp.int32, (32, 384), 0)
    col = lax.broadcasted_iota(jnp.int32, (32, 384), 1)
    tap_group = (col >> 2) - row - (LANES // 4 - reach)
    base = jnp.zeros((32, 384), jnp.float32)
    for group in range(TAPS // 4):
        base = jnp.where(tap_group == group, taps[group : group + 1, :], base)
    high = base.astype(jnp.bfloat16)
    low = (base - high.astype(jnp.float32)).astype(jnp.bfloat16)
    for block in range(rows // 32):
        span = slice(128 * block, 128 * block + 384)
        toep[0, 32 * block : 32 * block + 32, span] = high
        toep[1, 32 * block : 32 * block + 32, span] = low
    lead = LANES
    samples_in = raw[...]
    total = jnp.dot(toep[0, :, lead : lead + samples], samples_in, preferred_element_type=jnp.float32)
    total += jnp.dot(toep[1, :, lead : lead + samples], samples_in, preferred_element_type=jnp.float32)
    filtered = total.astype(jnp.bfloat16)
    channel = lax.broadcasted_iota(jnp.int32, (NSRC, channels), 1)
    pick = jnp.where(channel == ids[...], 1.0, 0.0).astype(jnp.bfloat16)
    picked = lax.dot_general(pick, filtered, NT, preferred_element_type=jnp.float32).astype(jnp.bfloat16)
    shift = jnp.full((8, LANES), offset[0] >> 2, jnp.int32).astype(jnp.float32)
    keep_rows = jnp.concatenate([jnp.broadcast_to(keep[...], (8, LANES)), shift], axis=0).astype(jnp.bfloat16)
    for owner in range(chans):
        blocks[owner, :used, :] = filtered[:used, owner * LANES : (owner + 1) * LANES]
        for tile in range(rows // LANES):
            at = used + tile * NSRC
            blocks[owner, at : at + NSRC, :] = picked[:, tile * LANES : (tile + 1) * LANES]
        blocks[owner, flag_row:, :] = keep_rows

    pl.semaphore_wait(barrier, chans + tms + cores - 3)

    sent = []

    def slot(part, owner):
        return out.at[part, owner]

    def send(source, part, owner, target):
        copy = pltpu.make_async_remote_copy(
            src_ref=source,
            dst_ref=slot(part, owner),
            send_sem=send_sem.at[len(sent)],
            recv_sem=recv_sem.at[part * chans + owner],
            device_id=target,
            device_id_type=pl.DeviceIdType.MESH,
        )
        copy.start()
        sent.append(copy)

    def arrive(part, owner):
        pltpu.make_async_remote_copy(
            src_ref=slot(part, owner),
            dst_ref=slot(part, owner),
            send_sem=send_sem.at[0],
            recv_sem=recv_sem.at[part * chans + owner],
            device_id={"chan": here},
            device_id_type=pl.DeviceIdType.MESH,
        ).wait_recv()

    def to_cores(part, owner):
        for step in range(1, cores):
            send(slot(part, owner), part, owner, {"src": lax.rem(core + step, cores)})

    for step in range(1, chans):
        there = lax.rem(here + step, chans)
        send(blocks.at[there], window, here, {"chan": there})
    own = pltpu.make_async_copy(blocks.at[here], slot(window, here), own_sem)
    own.start()
    for step in range(chans):
        owner = lax.rem(here + chans - step, chans)
        if step:
            arrive(window, owner)
        source = slot(window, owner) if step else blocks.at[here]
        for hop in range(1, tms):
            send(source, window, owner, {"tm": lax.rem(tm + hop, tms)})
        for turn in range(1, cores):
            send(source, window, owner, {"src": lax.rem(core + turn, cores)})
    own.wait()
    for step in range(chans):
        owner = lax.rem(here + chans - step, chans)
        for hop in range(1, tms):
            part = lax.rem(tm + tms - hop, tms) * cores + core
            arrive(part, owner)
            to_cores(part, owner)
    for step in range(chans):
        owner = lax.rem(here + chans - step, chans)
        for hop in range(tms):
            for turn in range(1, cores):
                part = lax.rem(tm + tms - hop, tms) * cores + lax.rem(core + turn, cores)
                arrive(part, owner)
    for copy in sent:
        copy.wait_send()


def correlate_kernel(sizes, samples, ids, keep, table, inverse, blocks, out, spec, src_spec, cross, joined, src_joined):
    chans, tms, cores = sizes
    windows = tms * cores
    count, reach, used, rows, flag_row = layout(samples)
    mine = NSRC // windows
    window = lax.axis_index("tm") * cores + lax.axis_index("src")
    width = 2 if windows % 2 == 0 else 1
    tiles = rows // LANES
    joined[...] = jnp.zeros_like(joined)
    src_joined[...] = jnp.zeros_like(src_joined)
    for owner in range(chans):
        at = slice(count * owner, count * owner + used)
        for part in range(windows):
            joined[part, at, :] += blocks[part, owner, :used, :].astype(jnp.float32)
        series = jnp.concatenate(
            [
                jnp.concatenate(
                    [blocks[part, owner, used + NSRC * tile : used + NSRC * (tile + 1), :] for tile in range(tiles)],
                    axis=1,
                )
                for part in range(windows)
            ],
            axis=0,
        ).astype(jnp.float32)
        src_joined[at, : windows * NSRC] += series.T[:used, :]
    starts = [
        jnp.max(blocks[part, 0, flag_row : flag_row + 16, :].astype(jnp.float32)[8:]).astype(jnp.int32) + reach
        for part in range(windows)
    ]
    for first in range(0, windows, width):
        lanes = slice(first * LANES, (first + width) * LANES)
        data = jnp.concatenate(
            [
                joined[part, pl.ds(starts[part], W), :].astype(jnp.bfloat16)
                for part in range(first, first + width)
            ],
            axis=1,
        )
        spec[:, lanes] = jnp.dot(table[...], data, preferred_element_type=jnp.float32)
    part_at = lax.broadcasted_iota(jnp.int32, (W, windows * NSRC), 1) // NSRC
    data = jnp.zeros((W, windows * NSRC), jnp.float32)
    for part in range(windows):
        data = jnp.where(part_at == part, src_joined[pl.ds(starts[part], W), :][:, : windows * NSRC], data)
    data = data.astype(jnp.bfloat16)
    src_spec[...] = jnp.dot(table[...], data, preferred_element_type=jnp.float32)

    channel = lax.broadcasted_iota(jnp.int32, (NSRC, LANES), 1)
    src_keep = jnp.zeros((NSRC, 1), jnp.float32)
    for owner in range(chans):
        flags = blocks[0, owner, flag_row : flag_row + 16, :].astype(jnp.float32)[:1]
        hit = channel + owner * LANES == ids[...]
        src_keep += jnp.sum(jnp.where(hit, flags, 0.0), axis=1, keepdims=True)
    number = lax.broadcasted_iota(jnp.int32, (NSRC, mine * LANES), 0)
    wanted = lax.broadcasted_iota(jnp.int32, (NSRC, mine * LANES), 1) // LANES + window * mine
    spread = (jnp.where(number == wanted, 1.0, 0.0) * src_keep).astype(jnp.bfloat16)
    keep_lanes = jnp.concatenate([keep[...]] * windows, axis=1)
    size = F // BANDS

    def whiten(real, imag, gain):
        power = jnp.mean(real * real + imag * imag, axis=0, keepdims=True)
        factor = gain / jnp.sqrt(power + 1e-06)
        return (real * factor).astype(jnp.bfloat16), (imag * factor).astype(jnp.bfloat16)

    @pl.loop(0, BANDS)
    def _(band):
        at_real = pl.ds(pl.multiple_of(band * size, size), size)
        at_imag = pl.ds(pl.multiple_of(F + band * size, size), size)
        real, imag = whiten(spec[at_real, :], spec[at_imag, :], keep_lanes)
        real, imag = real.astype(jnp.float32), imag.astype(jnp.float32)
        src = jnp.concatenate(
            whiten(src_spec[at_real, :], src_spec[at_imag, :], 1.0), axis=0
        )
        cross_real = [0.0] * mine
        cross_imag = [0.0] * mine
        for part in range(windows):
            wide = jnp.dot(
                src[:, part * NSRC : (part + 1) * NSRC], spread, preferred_element_type=jnp.float32
            )
            xr = real[:, part * LANES : (part + 1) * LANES]
            xi = imag[:, part * LANES : (part + 1) * LANES]
            for one in range(mine):
                sr = wide[:size, one * LANES : (one + 1) * LANES]
                si = wide[size:, one * LANES : (one + 1) * LANES]
                cross_real[one] = cross_real[one] + (sr * xr + si * xi)
                cross_imag[one] = cross_imag[one] + (sr * xi - si * xr)
        for one in range(mine):
            lanes = slice(one * LANES, (one + 1) * LANES)
            for at, value in ((at_real, cross_real[one]), (at_imag, cross_imag[one])):
                high = value.astype(jnp.bfloat16)
                cross[0, at, lanes] = high
                cross[1, at, lanes] = (value - high.astype(jnp.float32)).astype(jnp.bfloat16)

    scale = 1.0 / math.sqrt(windows * F)
    total = jnp.dot(inverse[...], cross[0], preferred_element_type=jnp.float32)
    total += jnp.dot(inverse[...], cross[1], preferred_element_type=jnp.float32)
    for one in range(mine):
        out[one] = total[:, one * LANES : (one + 1) * LANES] * scale


def body(sizes, table, inverse, raw_records, filter_taps, good_channels, source_ids, window_offsets):
    chans, tms, cores = sizes
    windows = tms * cores
    samples, channels = raw_records.shape[1:]
    count, reach, used, rows, flag_row = layout(samples)
    ids = source_ids.reshape(NSRC, 1)
    keep = good_channels.astype(jnp.float32).reshape(1, LANES)
    taps = jnp.tile(filter_taps.reshape(TAPS // 4, 4), (1, 96))
    vmem = pl.BlockSpec(memory_space=pltpu.VMEM)
    smem = pl.BlockSpec(memory_space=pltpu.SMEM)
    copies = chans - 1 + chans * (tms - 1 + cores - 1 + (tms - 1) * (cores - 1))
    gathered = pl.pallas_call(
        functools.partial(gather_kernel, sizes),
        out_shape=jax.ShapeDtypeStruct((windows, chans, flag_row + 16, LANES), jnp.bfloat16),
        in_specs=[smem, vmem, vmem, vmem, vmem],
        out_specs=vmem,
        scratch_shapes=[
            pltpu.VMEM((2, rows, 4 * rows + 256), jnp.bfloat16),
            pltpu.VMEM((chans, flag_row + 16, LANES), jnp.bfloat16),
            pltpu.SemaphoreType.DMA,
            pltpu.SemaphoreType.DMA((copies,)),
            pltpu.SemaphoreType.DMA((windows * chans,)),
        ],
        compiler_params=pltpu.CompilerParams(
            collective_id=0, has_side_effects=True, vmem_limit_bytes=VMEM_LIMIT
        ),
        cost_estimate=pl.CostEstimate(
            flops=4 * rows * samples * channels,
            bytes_accessed=2 * samples * channels + 2 * (copies + windows * chans) * (flag_row + 16) * LANES,
            transcendentals=0,
        ),
        name="gather",
    )(window_offsets, taps, ids, keep, raw_records.reshape(samples, channels))
    mine = NSRC // windows
    return pl.pallas_call(
        functools.partial(correlate_kernel, sizes, samples),
        out_shape=jax.ShapeDtypeStruct((mine, LAGS, LANES), jnp.float32),
        in_specs=[vmem] * 5,
        out_specs=vmem,
        scratch_shapes=[
            pltpu.VMEM((2 * F, windows * LANES), jnp.float32),
            pltpu.VMEM((2 * F, windows * NSRC), jnp.float32),
            pltpu.VMEM((2, 2 * F, mine * LANES), jnp.bfloat16),
            pltpu.VMEM((windows, up(count * (chans - 1) + used, 8), LANES), jnp.float32),
            pltpu.VMEM((up(count * (chans - 1) + used, 8), LANES), jnp.float32),
        ],
        compiler_params=pltpu.CompilerParams(vmem_limit_bytes=VMEM_LIMIT),
        name="correlate",
    )(ids, keep, table, inverse, gathered)


def solution(mesh):
    placed = (
        P(("groups", "tm", "src"), "chan", None),
        P(),
        P(("groups", "chan")),
        P("groups", None),
        P(("groups", "tm", "src")),
    )
    sizes = tuple(mesh.shape[name] for name in ("chan", "tm", "src"))

    def run(raw_records, *rest):
        return body(sizes, forward_rows(), inverse_rows(), raw_records, *rest)

    def call(raw_records, *rest):
        return jax.shard_map(
            run,
            mesh=mesh,
            in_specs=placed,
            out_specs=P(("groups", "tm", "src"), None, "chan"),
            check_vma=False,
        )(raw_records, *rest)

    return call
```
